32 devices in a mesh: wide: 16 (over z, x, core), narrow: 2 (over y).
Axes of the slice: x: 2, y: 2, z: 4, core: 2. Of those that a mesh axis runs over, the one named last changes fastest.
Arguments:
- tokens: bfloat16 [65536, 768], P(('wide', 'narrow')), may hold values from -6 to 6
- segments: int32 [65536], P(('wide', 'narrow')), may hold values from 0 to 3, as said below
- w_qkv: bfloat16 [768, 576], P(('wide', 'narrow')), may hold values from -0.4375 to 0.4375
- w_out: bfloat16 [768, 768], P(('wide', 'narrow')), may hold values from -1.75 to 1.75
- w_ff1: bfloat16 [768, 768], P(('wide', 'narrow')), may hold values from -0.4375 to 0.4375
- w_ff2: bfloat16 [3072, 192], P(('wide', 'narrow')), may hold values from -0.21875 to 0.21875
- gains: bfloat16 [2, 768], P(None, ('wide', 'narrow')), may hold values from 0.25 to 1.75
- biases: bfloat16 [10, 768], P(None, ('wide', 'narrow')), may hold values from -4 to 4
- cotangent: bfloat16 [65536, 768], P(('wide', 'narrow')), may hold values from -6 to 6
Outputs:
- layer_output: bfloat16 [65536, 768], P(('wide', 'narrow'))
- grad_tokens: bfloat16 [65536, 768], P(('wide', 'narrow'))
- grad_w_qkv: float32 [768, 576], P(('wide', 'narrow'))
- grad_w_out: float32 [768, 768], P(('wide', 'narrow'))
- grad_w_ff1: float32 [768, 768], P(('wide', 'narrow'))
- grad_w_ff2: float32 [3072, 192], P(('wide', 'narrow'))
- grad_gains: float32 [2, 768], P(None, ('wide', 'narrow'))
- grad_biases: float32 [10, 768], P(None, ('wide', 'narrow'))
The draws below stay inside these ranges and needn't reach their ends.
Inputs may be any that keep to these rules, and one draw needn't show every extreme that they name: `segments`: every aligned block of 512 tokens is either one sequence (all ids 0) or 4 sequences of 128 tokens, whose ids are the position within the block divided by 128; the first block is always of the second kind.
All inputs are finite; a program needn't handle non-finite values.
Results may differ from the reference program's by a relative error of at most 0.015.
Values may be sent and summed in bfloat16 or wider, within the bound.
No kernel may reach another device: no remote copies, remote signals or barrier semaphores. Data moves between devices by JAX's collectives and lax.ppermute only.
A program may use at most 192 MiB of HBM per device.

```python
import jax
import jax.numpy as jnp
from jax import lax

D = 768
HEADS = 12
HEAD_DIM = 64
FF = 3072
GROUPS = 4
SEQ_LEN = 512
SHORT_LEN = 128
TOKENS = 65536


def draw_segments(key, part):
    key = jax.random.fold_in(key, 11)
    block_count = TOKENS // SEQ_LEN
    kinds = jax.random.randint(key, (block_count,), 0, 5)
    single = (kinds > 0) & (jnp.arange(block_count) > 0)
    positions = jnp.arange(SEQ_LEN, dtype=jnp.int32) // SHORT_LEN
    ids = jnp.where(single[:, None], 0, positions[None, :])
    return ids.reshape(TOKENS).astype(jnp.int32)


def spiked(values, key, source, target, shards_of, factor):
    def block_of(axis_at):
        return (jnp.arange(values.shape[axis_at]) // (values.shape[axis_at] // shards_of)).reshape((-1,) + (1,) * (values.ndim - 1 - axis_at))

    first = jax.random.permutation(key, shards_of)[block_of(target)]
    second = (block_of(target) + shards_of // 2) % shards_of
    return jnp.where((block_of(source) == first) | (block_of(source) == second), factor * values, values)


def block_levels(stream_key, extent, pieces, smallest, high):
    level, own = 1.0, jax.random.fold_in(stream_key, 6)
    for dim, parts in pieces:
        draws = jnp.exp(jax.random.uniform(jax.random.fold_in(own, dim), (parts,), jnp.float32, smallest / len(pieces), high / len(pieces)))
        level = level * jnp.repeat(draws, extent[dim] // parts).reshape([-1 if axis == dim else 1 for axis in range(len(extent))])
    return level


def scatter_about(stream_key, shape, scale, limit, split=(), kind=jnp.bfloat16):
    level = block_levels(stream_key, shape, split, -0.22, 0.18) if split else 1.0
    drawn = jax.random.normal(stream_key, shape, jnp.float32) * scale * level
    return jnp.minimum(jnp.maximum(drawn, -limit), limit).astype(kind)


def gaussian_with(own_key, extent, spread, most, cuts, heavy, held_as=jnp.bfloat16):
    values = spread * jax.random.normal(own_key, extent, jnp.float32)
    if cuts:
        values = values * block_levels(own_key, extent, cuts, -0.22, 0.18)
    return jnp.clip(spiked(values, jax.random.fold_in(own_key, 3), *heavy), -most, most).astype(held_as)


def setup_inputs(seed: int = 0) -> dict:
    splits = jax.random.split(jax.random.key(seed), 10)
    tokens = scatter_about(splits[0], (TOKENS, D), 1.0, 6.0, ((0, 32),))
    segments = draw_segments(jax.random.fold_in(splits[9], 71), 0)
    w_qkv = scatter_about(splits[2], (D, 3 * D // GROUPS), (D // GROUPS) ** -0.5, 0.4375, ((0, 32),))
    w_out = scatter_about(splits[3], (D, D), (D // 64) ** -0.5, 1.75, ((0, 32),))
    w_ff1 = scatter_about(splits[4], (D, FF // GROUPS), (D // GROUPS) ** -0.5, 0.4375, ((0, 32),))
    w_ff2 = scatter_about(splits[5], (FF, D // GROUPS), (FF // GROUPS) ** -0.5, 0.21875, ((0, 32),))
    gains = jnp.clip(1.0 + 0.15 * jax.random.normal(splits[6], (2, D), jnp.float32), 0.25, 1.75).astype(jnp.bfloat16)
    biases = scatter_about(splits[7], (10, D), 0.3, 4.0, ((1, 32),))
    cotangent = gaussian_with(splits[8], (TOKENS, D), 1.0, 6.0, ((0, 32),), (0, 1, 32, 2.75))
    return dict(tokens=tokens, segments=segments, w_qkv=w_qkv, w_out=w_out, w_ff1=w_ff1, w_ff2=w_ff2, gains=gains, biases=biases, cotangent=cotangent)


@jax.custom_vjp
def low(v):
    return lax.optimization_barrier(v.astype(jnp.bfloat16)).astype(jnp.float32)

@jax.custom_vjp
def low_back(v):
    return v

def low_keep(v):
    return (low(v), None)

def low_pass(kept, grad):
    return (grad,)

def back_keep(v):
    return (v, None)

def back_low(kept, grad):
    return (low(grad),)
low.defvjp(low_keep, low_pass)
low_back.defvjp(back_keep, back_low)
highest = lax.Precision.HIGHEST
norm_eps = 1e-05
masked_score = -1e+30

def grouped_product(activations, weight):
    tok_count = activations.shape[0]
    width_in = weight.shape[0] // GROUPS
    split_rows = activations.reshape(tok_count, GROUPS, width_in)
    split_weight = weight.reshape(GROUPS, width_in, weight.shape[1])
    return jnp.einsum('ngc,gcd->ngd', split_rows, split_weight, precision=highest)

def layer_norm(values_in, gain, shift):
    average = lax.optimization_barrier(jnp.mean(values_in, axis=-1, keepdims=True))
    centred = values_in - average
    variance = lax.optimization_barrier(jnp.mean(centred * centred, axis=-1, keepdims=True))
    return centred * lax.rsqrt(variance + norm_eps) * gain + shift

def forward_rows(activations, seg_ids, w_qkv, w_out, w_ff1, w_ff2, gains, biases):
    tok_count = activations.shape[0]
    group_width = D // GROUPS
    blocks = tok_count // SEQ_LEN
    projected = grouped_product(activations, w_qkv)
    query = projected[:, :, :group_width].reshape(tok_count, D) + biases[0]
    keys = projected[:, :, group_width:2 * group_width].reshape(tok_count, D)
    values_all = projected[:, :, 2 * group_width:].reshape(tok_count, D) + biases[1]
    query = low(low_back(query)).reshape(blocks, SEQ_LEN, HEADS, HEAD_DIM)
    keys = low(low_back(keys)).reshape(blocks, SEQ_LEN, HEADS, HEAD_DIM)
    values_all = low(low_back(values_all)).reshape(blocks, SEQ_LEN, HEADS, HEAD_DIM)
    scores = jnp.einsum('bqhd,bkhd->bhqk', query, keys, precision=highest) * HEAD_DIM ** (-0.5)
    scores = low_back(scores)
    block_ids = seg_ids.reshape(blocks, SEQ_LEN)
    allowed = (block_ids[:, :, None] == block_ids[:, None, :])[:, None]
    scores = jnp.where(allowed, scores, masked_score)
    largest = lax.optimization_barrier(jnp.max(scores, axis=-1, keepdims=True))
    expon = jnp.exp(scores - largest)
    probs = low(expon / lax.optimization_barrier(jnp.sum(expon, axis=-1, keepdims=True)))
    mixed = jnp.einsum('bhqk,bkhd->bqhd', probs, values_all, precision=highest).reshape(tok_count, D)
    mixed = low(low_back(mixed))
    branch = low_back(jnp.dot(mixed, w_out, precision=highest) + biases[2])
    first = low(layer_norm(activations + branch, gains[0], biases[3]))
    hidden = grouped_product(first, w_ff1).reshape(tok_count, FF) + biases[4:8].reshape(FF)
    hidden = low(jax.nn.gelu(low_back(hidden), approximate=True))
    back = grouped_product(hidden, w_ff2).reshape(tok_count, D) + biases[8]
    back = low_back(back)
    return layer_norm(first + back, gains[1], biases[9])

def reference(tokens, segments, w_qkv, w_out, w_ff1, w_ff2, gains, biases, cotangent):
    params = tuple((weight.astype(jnp.float32) for weight in (w_qkv, w_out, w_ff1, w_ff2, gains, biases)))
    group_size = min(4096, TOKENS)
    group_count = TOKENS // group_size
    seg_groups = segments.reshape(group_count, group_size)

    def whole(activations, *weights):

        def one_group(item):
            return jax.checkpoint(forward_rows)(item[0], item[1], *weights)
        result = lax.map(one_group, (activations.reshape(group_count, group_size, D), seg_groups))
        return result.reshape(TOKENS, D)
    output, pullback = jax.vjp(whole, tokens.astype(jnp.float32), *params)
    grads = pullback(cotangent.astype(jnp.float32))
    return (output.astype(jnp.bfloat16), grads[0].astype(jnp.bfloat16), grads[1], grads[2], grads[3], grads[4], grads[5], grads[6])
```

```python
import functools
import jax
import jax.numpy as jnp
from jax import lax
from jax.sharding import PartitionSpec as P
from jax.experimental import pallas as pl
from jax.experimental.pallas import tpu as pltpu

D = 768; HEADS = 12; HEAD_DIM = 64; FF = 3072; GROUPS = 4; SEQ_LEN = 512
GW = D // GROUPS
WIN = 256
HPG = HEADS // GROUPS
EPS = 1e-5
BF = jnp.bfloat16; F32 = jnp.float32
VMEM = 60 * 1024 * 1024

def dot_nn(a, b): return lax.dot_general(a, b, (((1,), (0,)), ((), ())), preferred_element_type=F32)
def dot_nt(a, b): return lax.dot_general(a, b, (((1,), (1,)), ((), ())), preferred_element_type=F32)
def dot_tn(a, b): return lax.dot_general(a, b, (((0,), (0,)), ((), ())), preferred_element_type=F32)

def halves(x):
    lane = lax.broadcasted_iota(jnp.int32, x.shape, 1)
    zero = jnp.zeros_like(x)
    return jnp.where(lane < HEAD_DIM, x, zero), jnp.where(lane < HEAD_DIM, zero, x)

def load_package(g, w, wp, bp):
    @pl.when(pl.program_id(1) == 0)
    def _():
        count, rows = w.shape[1], w.shape[2] - 1
        pieces = [w[0, d].astype(F32) for d in range(count)]
        mat = jnp.concatenate([piece[:rows] for piece in pieces], axis=0).astype(BF)
        start = pl.multiple_of(64 * (g % 2), 64)
        wp[pl.ds(pl.multiple_of(GW - GW * (g % 2), 64), WIN - GW), :] = jnp.zeros((WIN - GW, 3 * WIN), BF)
        wp[pl.ds(start, GW), :] = mat
        row = pieces[0][rows:]
        for piece in pieces[1:]:
            row = row + piece[rows:]
        bp[0:1, :] = row

def attn_fwd_kernel(gidx, seg, t0, t1, w, qkv_out, p_out, mix_out, wp, bp):
    i = pl.program_id(1)
    load_package(gidx[pl.program_id(0)], w, wp, bp)
    x = jnp.concatenate([t0[...], t1[...]], axis=1)
    proj = dot_nn(x, wp[...]) + bp[0:1, :]
    q = proj[:, :WIN].astype(BF) * BF(HEAD_DIM ** -0.5)
    k = proj[:, WIN:2 * WIN].astype(BF)
    v = proj[:, 2 * WIN:].astype(BF)
    qkv_out[0, :, :WIN] = q
    qkv_out[0, :, WIN:2 * WIN] = k
    qkv_out[0, :, 2 * WIN:] = v
    v_t = v.T
    k_lo, k_hi = halves(k[:, :128])
    k_heads = (k_lo, k_hi, k[:, 128:])
    q_tiles = (q[:, :128], q[:, :128], q[:, 128:])

    def heads(short):
        outs = []
        if short:
            rows = lax.broadcasted_iota(jnp.int32, (SEQ_LEN, SEQ_LEN), 0) // 128
            cols = lax.broadcasted_iota(jnp.int32, (SEQ_LEN, SEQ_LEN), 1) // 128
            allowed = rows == cols
        for h in range(HPG):
            s = dot_nt(k_heads[h], q_tiles[h])
            if short:
                s = jnp.where(allowed, s, -1e30)
            e = jnp.exp(s - jnp.max(s, axis=0, keepdims=True))
            p = (e * (1.0 / jnp.sum(e, axis=0, keepdims=True))).astype(BF)
            p_out[0, h, 0] = p
            outs.append(dot_nn(v_t[h * HEAD_DIM:(h + 1) * HEAD_DIM, :], p))
        outs.append(jnp.zeros((WIN - GW, SEQ_LEN), F32))
        mix_out[0] = jnp.concatenate(outs, axis=0).T.astype(BF)

    is_short = seg[i * SEQ_LEN + SEQ_LEN - 1] != 0

    @pl.when(is_short)
    def _():
        heads(True)

    @pl.when(jnp.logical_not(is_short))
    def _():
        heads(False)

def tile0(g): return 3 * (g // 2) + g % 2

def attn_fwd(gidx, segments, tokens, wq):
    ng = gidx.shape[0]; tcount = tokens.shape[0]; nb = tcount // SEQ_LEN
    return pl.pallas_call(
        attn_fwd_kernel,
        grid_spec=pltpu.PrefetchScalarGridSpec(
            num_scalar_prefetch=2, grid=(ng, nb),
            in_specs=[
                pl.BlockSpec((SEQ_LEN, 128), lambda j, i, g, s: (i, tile0(g[j]))),
                pl.BlockSpec((SEQ_LEN, 128), lambda j, i, g, s: (i, tile0(g[j]) + 1)),
                pl.BlockSpec((1,) + wq.shape[1:], lambda j, i, g, s: (j, 0, 0, 0)),
            ],
            out_specs=[
                pl.BlockSpec((1, SEQ_LEN, 3 * WIN), lambda j, i, g, s: (j, i, 0)),
                pl.BlockSpec((1, HPG, 1, SEQ_LEN, SEQ_LEN), lambda j, i, g, s: (j, 0, i, 0, 0)),
                pl.BlockSpec((1, SEQ_LEN, WIN), lambda j, i, g, s: (j, i, 0)),
            ],
            scratch_shapes=[pltpu.VMEM((WIN, 3 * WIN), BF), pltpu.VMEM((8, 3 * WIN), F32)]),
        out_shape=[
            jax.ShapeDtypeStruct((ng, tcount, 3 * WIN), BF),
            jax.ShapeDtypeStruct((ng, HPG, nb, SEQ_LEN, SEQ_LEN), BF),
            jax.ShapeDtypeStruct((ng, tcount, WIN), BF),
        ],
        compiler_params=pltpu.CompilerParams(vmem_limit_bytes=VMEM),
        name="attn_fwd",
    )(gidx, segments, tokens, tokens, wq)

def attn_bwd_kernel(gidx, t0, t1, w, qkv, p_in, dmix, mix, dtok_out, gw_out, gb_out, wp, bp):
    i = pl.program_id(1)
    load_package(gidx[pl.program_id(0)], w, wp, bp)
    x = jnp.concatenate([t0[...], t1[...]], axis=1)
    q = qkv[0, :, :WIN]; k = qkv[0, :, WIN:2 * WIN]; v = qkv[0, :, 2 * WIN:]
    d_o = dmix[0]
    k_t = k.T
    prod = d_o.astype(F32) * mix[0].astype(F32)
    prod_hi = prod.astype(BF)
    prod_lo = (prod - prod_hi.astype(F32)).astype(BF)
    sel = (lax.broadcasted_iota(jnp.int32, (8, WIN), 0) == lax.broadcasted_iota(jnp.int32, (8, WIN), 1) // HEAD_DIM).astype(F32).astype(BF)
    delta = dot_nt(sel, prod_hi) + dot_nt(sel, prod_lo)
    v_lo, v_hi = halves(v[:, :128])
    v_heads = (v_lo, v_hi, v[:, 128:])
    lane_low = lax.broadcasted_iota(jnp.int32, (SEQ_LEN, 128), 1) < HEAD_DIM
    dks, dvs, dqs = [], [], []
    for h in range(HPG):
        tile = slice(128 * (h // 2), 128 * (h // 2) + 128)
        p = p_in[0, h, 0]
        dp = dot_nt(v_heads[h], d_o[:, tile])
        ds = (p.astype(F32) * (dp - delta[h:h + 1, :])).astype(BF)
        dvs.append(dot_nn(p, d_o[:, tile]))
        dks.append(dot_nn(ds, q[:, tile]))
        dqs.append(dot_nn(k_t[h * HEAD_DIM:(h + 1) * HEAD_DIM, :], ds))
    dqs.append(jnp.zeros((WIN - GW, SEQ_LEN), F32))
    dq = (jnp.concatenate(dqs, axis=0).T * (HEAD_DIM ** -0.5)).astype(BF)
    dk = jnp.concatenate([jnp.where(lane_low, dks[0], dks[1]), dks[2]], axis=1).astype(BF)
    dv = jnp.concatenate([jnp.where(lane_low, dvs[0], dvs[1]), dvs[2]], axis=1).astype(BF)
    dproj = jnp.concatenate([dq, dk, dv], axis=1)
    dtok_out[0] = dot_nt(dproj, wp[...]).astype(BF)
    gw = dot_tn(x, dproj)
    gq = jnp.sum(dq.astype(F32), axis=0, keepdims=True)
    gv = jnp.sum(dv.astype(F32), axis=0, keepdims=True)
    gb = jnp.concatenate([gq, gv, jnp.zeros((6, WIN), F32)], axis=0)

    @pl.when(i == 0)
    def _():
        gw_out[0] = gw
        gb_out[0] = gb

    @pl.when(i > 0)
    def _():
        gw_out[0] += gw
        gb_out[0] += gb

def attn_bwd(gidx, tokens, wq, qkv, probs, dmix, mix):
    ng = gidx.shape[0]; tcount = tokens.shape[0]; nb = tcount // SEQ_LEN
    return pl.pallas_call(
        attn_bwd_kernel,
        grid_spec=pltpu.PrefetchScalarGridSpec(
            num_scalar_prefetch=1, grid=(ng, nb),
            in_specs=[
                pl.BlockSpec((SEQ_LEN, 128), lambda j, i, g: (i, tile0(g[j]))),
                pl.BlockSpec((SEQ_LEN, 128), lambda j, i, g: (i, tile0(g[j]) + 1)),
                pl.BlockSpec((1,) + wq.shape[1:], lambda j, i, g: (j, 0, 0, 0)),
                pl.BlockSpec((1, SEQ_LEN, 3 * WIN), lambda j, i, g: (j, i, 0)),
                pl.BlockSpec((1, HPG, 1, SEQ_LEN, SEQ_LEN), lambda j, i, g: (j, 0, i, 0, 0)),
                pl.BlockSpec((1, SEQ_LEN, WIN), lambda j, i, g: (g[j], i, 0)),
                pl.BlockSpec((1, SEQ_LEN, WIN), lambda j, i, g: (j, i, 0)),
            ],
            out_specs=[
                pl.BlockSpec((1, SEQ_LEN, WIN), lambda j, i, g: (j, i, 0)),
                pl.BlockSpec((1, WIN, 3 * WIN), lambda j, i, g: (j, 0, 0)),
                pl.BlockSpec((1, 8, WIN), lambda j, i, g: (j, 0, 0)),
            ],
            scratch_shapes=[pltpu.VMEM((WIN, 3 * WIN), BF), pltpu.VMEM((8, 3 * WIN), F32)]),
        out_shape=[
            jax.ShapeDtypeStruct((ng, tcount, WIN), BF),
            jax.ShapeDtypeStruct((ng, WIN, 3 * WIN), F32),
            jax.ShapeDtypeStruct((ng, 8, WIN), F32),
        ],
        compiler_params=pltpu.CompilerParams(vmem_limit_bytes=VMEM),
        name="attn_bwd",
    )(gidx, tokens, tokens, wq, qkv, probs, dmix, mix)

C0 = 0.7978845608028654
C1 = C0 * 0.044715

def assemble(ws):
    parts = []
    for p in range(GROUPS // 2):
        a, b = ws[2 * p], ws[2 * p + 1]
        parts += [a[:, :128], a[:, 128:] + b[:, :128], b[:, 128:]]
    return jnp.concatenate(parts, axis=1)

def rowmean(v): return jnp.sum(v, axis=1, keepdims=True) * (1.0 / D)
def colsum(v): return jnp.sum(v.astype(F32), axis=0, keepdims=True)

def mid_kernel(tok, cot, m0, m1, m2, m3, wx, w2, gains, biases,
               out, dmix, dres_out, gx, gy, small,
               w1p, w2p, wop, acc_o, acc1, acc2, hid, gp):
    i = pl.program_id(0)

    @pl.when(i == 0)
    def _():
        zr = jnp.zeros((WIN - GW, D), BF)
        per_group = wx.shape[0] // GROUPS
        rows = wx.shape[1]
        for g in range(GROUPS):
            o = 64 * (g % 2)
            both = jnp.concatenate([wx[per_group * g + d].astype(F32) for d in range(per_group)], axis=0).astype(BF)
            w1p[g, o:o + GW, :] = both[:, D:]
            w1p[g, (0 if o else GW):(o if o else WIN), :] = zr
            wop[g, :GW, :] = both[:, :D]
            wop[g, GW:, :] = zr
            z2 = jnp.zeros((D, WIN - GW), BF)
            blk = w2[D * g:D * (g + 1), :]
            w2p[g] = jnp.concatenate([z2, blk] if o else [blk, z2], axis=1)
        acc_o[...] = jnp.zeros_like(acc_o)
        acc1[...] = jnp.zeros_like(acc1)
        acc2[...] = jnp.zeros_like(acc2)
        small[...] = jnp.zeros_like(small)

    def win(v, g):
        s = 128 * tile0(g)
        return v[:, s:s + WIN]

    mix = (m0, m1, m2, m3)
    gain = gains[...]
    bias = biases[...]
    branch = dot_nn(mix[0][0], wop[0])
    for g in range(1, GROUPS):
        branch += dot_nn(mix[g][0], wop[g])
    r1 = tok[...].astype(F32) + branch + bias[2:3]
    r1 = r1 - rowmean(r1)
    rs1 = lax.rsqrt(rowmean(r1 * r1) + EPS)
    xh1 = r1 * rs1
    f16 = (xh1 * gain[0:1] + bias[3:4]).astype(BF)
    backs = []
    for g in range(GROUPS):
        u = dot_nn(win(f16, g), w1p[g]) + bias[4 + g:5 + g]
        s = u * u
        t = jnp.tanh(u * (C0 + C1 * s))
        h = 0.5 * t + 0.5
        a = u * h
        gp[g] = (h + a * (1.0 - h) * (2 * C0 + 6 * C1 * s)).astype(BF)
        a16 = a.astype(BF)
        hid[g] = a16
        backs.append(dot_nn(a16, w2p[g]))
    r2 = f16.astype(F32) + assemble(backs) + bias[8:9]
    r2 = r2 - rowmean(r2)
    rs2 = lax.rsqrt(rowmean(r2 * r2) + EPS)
    xh2 = r2 * rs2
    out[...] = (xh2 * gain[1:2] + bias[9:10]).astype(BF)
    c = cot[...].astype(F32)
    gg2 = colsum(c * xh2)
    gs2 = colsum(c)
    e = c * gain[1:2]
    d2 = rs2 * (e - rowmean(e) - xh2 * rowmean(e * xh2))
    db = d2.astype(BF)
    gb8 = colsum(db)
    dfs, gbf = [], []
    for g in range(GROUPS):
        dbw = win(db, g)
        dpre = (dot_nt(dbw, w2p[g]) * gp[g].astype(F32)).astype(BF)
        gbf.append(colsum(dpre))
        acc2[g] += dot_tn(hid[g], dbw)
        acc1[g] += dot_tn(win(f16, g), dpre)
        dfs.append(dot_nt(dpre, w1p[g]))
    df = d2 + assemble(dfs)
    gg1 = colsum(df * xh1)
    gs1 = colsum(df)
    e = df * gain[0:1]
    dres = rs1 * (e - rowmean(e) - xh1 * rowmean(e * xh1))
    dbr = dres.astype(BF)
    dres_out[...] = dbr
    gb2 = colsum(dbr)
    for g in range(GROUPS):
        acc_o[g] += dot_tn(mix[g][0], dbr)
        dmix[g] = dot_nt(dbr, wop[g]).astype(BF)
    z = jnp.zeros((1, D), F32)
    small[...] += jnp.concatenate([gg1, gg2, z, z, gb2, gs1] + gbf + [gb8, gs2, z, z, z, z], axis=0)

    @pl.when(i == pl.num_programs(0) - 1)
    def _():
        for g in range(GROUPS):
            o = 64 * (g % 2)
            gx[GW * g:GW * (g + 1), :D] = acc_o[g, :GW, :].astype(BF)
            gx[GW * g:GW * (g + 1), D:] = acc1[g, o:o + GW, :].astype(BF)
            gy[D * g:D * (g + 1), :] = acc2[g][:, o:o + GW].astype(BF)

def mid(tokens, cot, mix, wx, w2, gains, biases, tb=SEQ_LEN):
    tcount = tokens.shape[0]; n = tcount // tb
    whole = lambda s: pl.BlockSpec(s, lambda i: (0,) * len(s), pipeline_mode=pl.Buffered(1))
    return pl.pallas_call(
        mid_kernel,
        grid=(n,),
        in_specs=[
            pl.BlockSpec((tb, D), lambda i: (i, 0)),
            pl.BlockSpec((tb, D), lambda i: (i, 0)),
        ] + [pl.BlockSpec((1, tb, WIN), lambda i: (0, i, 0))] * GROUPS + [
            whole(wx.shape), whole((FF, GW)), whole((2, D)), whole((10, D)),
        ],
        out_specs=[
            pl.BlockSpec((tb, D), lambda i: (i, 0)),
            pl.BlockSpec((GROUPS, tb, WIN), lambda i: (0, i, 0)),
            pl.BlockSpec((tb, D), lambda i: (i, 0)),
            whole((D, 2 * D)), whole((FF, GW)), whole((16, D)),
        ],
        out_shape=[
            jax.ShapeDtypeStruct((tcount, D), BF),
            jax.ShapeDtypeStruct((GROUPS, tcount, WIN), BF),
            jax.ShapeDtypeStruct((tcount, D), BF),
            jax.ShapeDtypeStruct((D, 2 * D), BF),
            jax.ShapeDtypeStruct((FF, GW), BF),
            jax.ShapeDtypeStruct((16, D), F32),
        ],
        scratch_shapes=[
            pltpu.VMEM((GROUPS, WIN, D), BF), pltpu.VMEM((GROUPS, D, WIN), BF), pltpu.VMEM((GROUPS, WIN, D), BF),
            pltpu.VMEM((GROUPS, WIN, D), F32), pltpu.VMEM((GROUPS, WIN, D), F32), pltpu.VMEM((GROUPS, D, WIN), F32),
            pltpu.VMEM((GROUPS, tb, D), BF), pltpu.VMEM((GROUPS, tb, D), BF),
        ],
        compiler_params=pltpu.CompilerParams(vmem_limit_bytes=VMEM),
        name="mid",
    )(tokens, cot, *mix, wx, w2, gains, biases)


AXES = ("wide", "narrow")


def exchange(x, count, bit):
    return lax.ppermute(x, AXES, [(i, i ^ (1 << bit)) for i in range(count)])


def gather_bits(shard, me, count, order):
    bits = count.bit_length() - 1
    buf = shard.reshape((1,) * bits + shard.shape)
    for bit in order:
        axis = bits - 1 - bit
        other = exchange(buf, count, bit)
        mine_first = ((me >> bit) & 1) == 0
        buf = jnp.where(
            mine_first, jnp.concatenate([buf, other], axis), jnp.concatenate([other, buf], axis)
        )
    return buf.reshape((count,) + shard.shape)


def scatter_bits(parts, me, count, order):
    bits = count.bit_length() - 1
    tail = parts.shape[1:]
    buf = parts.reshape((2,) * bits + tail)
    for step, bit in enumerate(order):
        axis = bits - 1 - bit
        mine = (me >> bit) & 1
        keep = lax.dynamic_slice_in_dim(buf, mine, 1, axis)
        other = exchange(lax.dynamic_slice_in_dim(buf, 1 - mine, 1, axis), count, bit)
        buf = keep.astype(F32) + other.astype(F32)
        if step + 1 < len(order):
            buf = buf.astype(BF)
    return buf.reshape(tail)


def per_device(tokens, segments, w_qkv, w_out, w_ff1, w_ff2, gains, biases, cotangent, wide, narrow):
    count = wide * narrow
    bits = count.bit_length() - 1
    core = narrow.bit_length() - 1
    me = lax.axis_index(AXES)
    rows = w_qkv.shape[0]
    cols = gains.shape[1]
    per_group = count // GROUPS
    high = [b for b in range(bits - 1, -1, -1) if b != core]
    order_a = high + [core]
    order_b = high[:-2] + [high[-1], high[-2], core]

    padded = jnp.pad(w_qkv.reshape(rows, 3, GW), ((0, 0), (0, 0), (0, WIN - GW))).reshape(rows, 3 * WIN)
    place = cols * (me % per_group)
    bias_row = jnp.zeros((1, 3 * WIN), BF)
    bias_row = lax.dynamic_update_slice(bias_row, biases[0:1], (0, place))
    bias_row = lax.dynamic_update_slice(bias_row, biases[1:2], (0, 2 * WIN + place))
    package = gather_bits(jnp.concatenate([padded, bias_row]), me, count, order_a)
    package = package.reshape(GROUPS, per_group, rows + 1, 3 * WIN)
    if rows % 8:
        mats = package[:, :, :rows].reshape(GROUPS, GW, 3 * WIN)
        tops = jnp.sum(package[:, :, rows:].astype(F32), axis=1).astype(BF)
        package = jnp.concatenate([mats, tops], axis=1)[:, None]

    gate_row = jnp.pad(jnp.concatenate([gains, biases]).reshape(1, 12 * cols), ((0, 0), (0, 2 * D - 12 * cols)))
    mats = gather_bits(jnp.concatenate([jnp.concatenate([w_out, w_ff1], axis=1), gate_row]), me, count, order_a)
    w_two = gather_bits(w_ff2, me, count, order_b).reshape(FF, GW)
    vectors = mats[:, rows, : 12 * cols].reshape(count, 12, cols).transpose(1, 0, 2).reshape(12, D).astype(F32)
    mats = mats[:, :rows]
    if rows % 8:
        mats = mats.reshape(GROUPS, GW, 2 * D)

    forward = []
    for g in range(GROUPS):
        forward.append(attn_fwd(jnp.full((1,), g, jnp.int32), segments, tokens, package[g : g + 1]))
    mixes = [f[2] for f in forward]
    out, dmix, dres, grad_x, grad_two, small = mid(tokens, cotangent, mixes, mats, w_two, vectors[:2], vectors[2:])
    windows, grads, tops = [], [], []
    for g in range(GROUPS):
        qkv, probs, mix = forward[g]
        dtok, gw, gb = attn_bwd(jnp.full((1,), g, jnp.int32), tokens, package[g : g + 1], qkv, probs, dmix, mix)
        windows.append(dtok[0].astype(F32))
        start = 64 * (g % 2)
        grads.append(gw[0, start : start + GW].astype(BF))
        tops.append(gb[0, :2, :GW])
    rev_a, rev_b = order_a[::-1], order_b[::-1]
    shard_x = scatter_bits(grad_x.reshape(count, rows, 2 * D), me, count, rev_a)
    shard_two = scatter_bits(grad_two.reshape(count, FF // count, GW), me, count, rev_b)
    grad_tokens = (dres.astype(F32) + assemble(windows)).astype(BF)
    small = jnp.concatenate([small[:2], jnp.concatenate(tops, axis=1), small[4:12]])
    small = small.reshape(12, count, cols).transpose(1, 0, 2).reshape(count, 1, 12 * cols).astype(BF)
    small = jnp.pad(small, ((0, 0), (0, 0), (0, 3 * WIN - 12 * cols)))
    grad_qkv = jnp.concatenate([jnp.concatenate(grads).reshape(count, rows, 3 * WIN), small], axis=1)
    shard_qkv = scatter_bits(grad_qkv, me, count, rev_a)
    vec = shard_qkv[rows, : 12 * cols].reshape(12, cols)
    shard_qkv = shard_qkv[:rows].reshape(rows, 3, WIN)[:, :, :GW].reshape(rows, 3 * GW)
    return out, grad_tokens, shard_qkv, shard_x[:, :D], shard_x[:, D:], shard_two, vec[:2], vec[2:]


def solution(mesh):
    both = P(AXES, None)
    last = P(None, AXES)
    body = functools.partial(per_device, wide=mesh.shape["wide"], narrow=mesh.shape["narrow"])
    return jax.shard_map(
        body,
        mesh=mesh,
        in_specs=(both, P(AXES), both, both, both, both, last, last, both),
        out_specs=(both, both, both, both, both, both, last, last),
        check_vma=False,
    )
```
